32 devices in a mesh: groups: 2 (over y), row: 4 (over x, core), col: 4 (over z).
Axes of the slice: x: 2, y: 2, z: 4, core: 2. Of those that a mesh axis runs over, the one named last changes fastest.
Arguments:
- tokens: bfloat16 [1024, 4096], P(('groups', 'col'), 'row'), parts along dimension 0, may hold values from -6 to 6
- cotangent: bfloat16 [1024, 4096], P(('groups', 'col'), 'row'), parts along dimension 0, may hold values from -3 to 3
- gate_weight: bfloat16 [4096, 16384], P('row', 'col'), may hold values from -0.125 to 0.125
- up_weight: bfloat16 [4096, 16384], P('row', 'col'), may hold values from -0.125 to 0.125
- down_weight: bfloat16 [16384, 4096], P('col', 'row'), may hold values from -0.0625 to 0.0625
- gate_keep: int32 [32, 128], P('row', 'col'), may hold values from 0 to 1, as said below
- down_keep: int32 [128, 32], P('col', 'row'), may hold values from 0 to 1, as said below
Outputs:
- token_gradient: bfloat16 [1024, 4096], P(('groups', 'col'), 'row'), parts along dimension 0
- gate_gradient: bfloat16 [8192, 16384], P(('groups', 'row'), 'col'), parts along dimension 0
- up_gradient: bfloat16 [8192, 16384], P(('groups', 'row'), 'col'), parts along dimension 0
- down_gradient: bfloat16 [32768, 4096], P(('groups', 'col'), 'row'), parts along dimension 0
The draws below stay inside these ranges and needn't reach their ends.
There are 2 independent parts, one for each index of `groups`. The reference program is written for one: setup_inputs(seed, part) draws one part's arguments, and reference() takes and returns one part's arrays. A program takes and returns all parts, laid end to end along the dimension named above; an argument that names none is the same for every part. Nothing has to cross between parts.
Inputs may be any that keep to these rules, and one draw needn't show every extreme that they name: `gate_keep`: exactly half of the entries are 1 (block kept), the others 0. `down_keep`: exactly half of the entries are 1 (block kept), the others 0.
All inputs are finite; a program needn't handle non-finite values.
Results may differ from the reference program's by a relative error of at most 0.019.
Values may be sent and summed in bfloat16 or wider, within the bound.
A program may use at most 192 MiB of HBM per device.

```python
import jax
import jax.numpy as jnp
from jax import lax

D = 4096
F = 16384
BLK = 128
TOKENS = 512
DB = 32
FB = 128
N_ROW = 4
N_COL = 4


def half_mask(key, height, breadth):
    order = jax.random.permutation(key, height * breadth)
    return (order < height * breadth // 2).astype(jnp.int32).reshape(height, breadth)


def draw_gate_keep(key, part):
    key = jax.random.fold_in(key, 11)
    return half_mask(key, DB, FB)


def draw_down_keep(key, part):
    key = jax.random.fold_in(key, 23)
    return half_mask(key, FB, DB)


def steps_of(rng, extent, shards, least, largest):
    level = 1.0
    for axis_at, shards_of in shards:
        heights = jax.random.uniform(jax.random.fold_in(jax.random.fold_in(rng, 6), axis_at), (shards_of,), jnp.float32, least / len(shards), largest / len(shards))
        level = level * jnp.repeat(jnp.exp(heights), extent[axis_at] // shards_of).reshape((-1,) + (1,) * (len(extent) - 1 - axis_at))
    return level


def centred(rng, shape, spread, limit, cuts=(), dtype=jnp.bfloat16):
    result = jax.random.normal(rng, shape, jnp.float32) * spread
    if len(cuts) > 0:
        result = steps_of(rng, shape, cuts, -0.22, 0.18) * result
    return jnp.clip(result, min=-limit, max=limit).astype(dtype)


def setup_inputs(seed: int = 0, part: int = 0) -> dict:
    splits = jax.random.split(jax.random.key(seed), 8)
    part_keys = jax.random.split(jax.random.fold_in(splits[7], part), 8)
    tokens = centred(part_keys[0], (TOKENS, D), 1.0, 6.0, ((0, 4), (1, 4)))
    cotangent = centred(part_keys[1], (TOKENS, D), 0.5, 3.0, ((0, 4), (1, 4)))
    gate_weight = centred(splits[2], (D, F), (D // 2) ** -0.5, 0.125, ((0, 4), (1, 4)))
    up_weight = centred(splits[3], (D, F), (D // 2) ** -0.5, 0.125, ((0, 4), (1, 4)))
    down_weight = centred(splits[4], (F, D), (F // 2) ** -0.5, 0.0625, ((0, 4), (1, 4)))
    gate_keep = draw_gate_keep(jax.random.fold_in(splits[7], 71), part)
    down_keep = draw_down_keep(jax.random.fold_in(splits[7], 71), part)
    return dict(tokens=tokens, cotangent=cotangent, gate_weight=gate_weight, up_weight=up_weight, down_weight=down_weight, gate_keep=gate_keep, down_keep=down_keep)


def expand_mask(keep):
    return jnp.repeat(jnp.repeat(keep, BLK, axis=0), BLK, axis=1).astype(jnp.bfloat16)


def rounded(value):
    return lax.optimization_barrier(value.astype(jnp.bfloat16)).astype(jnp.float32)


def reference(tokens, cotangent, gate_weight, up_weight, down_weight, gate_keep, down_keep):
    gate_mask = expand_mask(gate_keep)
    down_mask = expand_mask(down_keep)
    gate_kept = gate_weight * gate_mask
    up_kept = up_weight * gate_mask
    down_kept = down_weight * down_mask
    band = D // N_ROW
    gate = jnp.zeros((TOKENS, F), jnp.float32)
    up = jnp.zeros((TOKENS, F), jnp.float32)
    hidden_delta = jnp.zeros((TOKENS, F), jnp.float32)
    for piece in range(N_ROW):
        lower = piece * band
        token_band = tokens[:, lower:lower + band]
        cotangent_band = cotangent[:, lower:lower + band]
        gate = gate + rounded(jnp.dot(token_band, gate_kept[lower:lower + band], preferred_element_type=jnp.float32))
        up = up + rounded(jnp.dot(token_band, up_kept[lower:lower + band], preferred_element_type=jnp.float32))
        hidden_delta = hidden_delta + rounded(jnp.dot(cotangent_band, down_kept[:, lower:lower + band].T, preferred_element_type=jnp.float32))
    hidden = (jax.nn.silu(gate) * up).astype(jnp.bfloat16)
    sigma = jax.nn.sigmoid(gate)
    gate_delta = (hidden_delta * up * sigma * (1.0 + gate * (1.0 - sigma))).astype(jnp.bfloat16)
    up_delta = (hidden_delta * gate * sigma).astype(jnp.bfloat16)
    down_gradient = (jnp.dot(hidden.T, cotangent, preferred_element_type=jnp.float32) * down_mask.astype(jnp.float32)).astype(jnp.bfloat16)
    gate_gradient = (jnp.dot(tokens.T, gate_delta, preferred_element_type=jnp.float32) * gate_mask.astype(jnp.float32)).astype(jnp.bfloat16)
    up_gradient = (jnp.dot(tokens.T, up_delta, preferred_element_type=jnp.float32) * gate_mask.astype(jnp.float32)).astype(jnp.bfloat16)
    span = F // N_COL
    token_gradient = jnp.zeros((TOKENS, D), jnp.float32)
    for piece in range(N_COL):
        lower = piece * span
        term = jnp.dot(gate_delta[:, lower:lower + span], gate_kept[:, lower:lower + span].T, preferred_element_type=jnp.float32)
        term = term + jnp.dot(up_delta[:, lower:lower + span], up_kept[:, lower:lower + span].T, preferred_element_type=jnp.float32)
        token_gradient = token_gradient + rounded(term)
    return token_gradient.astype(jnp.bfloat16), gate_gradient, up_gradient, down_gradient
```

```python
import functools

import jax
import jax.numpy as jnp
from jax import lax
from jax.experimental import pallas as pl
from jax.experimental.pallas import tpu as pltpu
from jax.sharding import PartitionSpec as P

BLK = 128
CONTRACT_ROWS = (((0,), (0,)), ((), ()))
CONTRACT_COLUMNS = (((1,), (1,)), ((), ()))


def widen(keep, axis):
    return jnp.repeat(keep, BLK, axis=axis).astype(jnp.bfloat16)


def masked(weight, lines):
    rows, columns = weight.shape
    blocked = weight.reshape(rows // BLK, BLK, columns) * lines[:, None, :]
    return blocked.reshape(rows, columns)


def ahead(left, weight):
    return jnp.dot(left, weight, preferred_element_type=jnp.float32)


def behind(left, weight):
    return lax.dot_general(left, weight, CONTRACT_COLUMNS, preferred_element_type=jnp.float32)


def outer(left, right):
    return lax.dot_general(left, right, CONTRACT_ROWS, preferred_element_type=jnp.float32)


def deltas(total):
    gate, up, hidden_delta = total[0], total[1], total[2]
    sigma = jax.nn.sigmoid(gate)
    active = gate * sigma
    hidden = active * up
    gate_delta = hidden_delta * up * sigma * (1.0 + gate * (1.0 - sigma))
    up_delta = hidden_delta * active
    return jnp.stack([hidden, gate_delta, up_delta]).astype(jnp.bfloat16)


def gradient_kernel(flip, left_ref, right_ref, mask_ref, *refs):
    out_ref = refs[-1]
    if flip:
        product = outer(left_ref[...], right_ref[...])
    else:
        product = ahead(left_ref[...], right_ref[...])
    rows, columns = product.shape
    blocked = product.reshape(rows // BLK, BLK, columns) * mask_ref[...].reshape(rows // BLK, 1, columns)
    out_ref[...] = blocked.reshape(rows, columns).astype(out_ref.dtype)


def column_gradient(rows_t, delta, mask, into, shape, first):
    height, depth = rows_t.shape
    width = delta.shape[1]
    step = min(256, width)
    base = first // step
    extra = [] if into is None else [into]
    return pl.pallas_call(
        functools.partial(gradient_kernel, False),
        out_shape=jax.ShapeDtypeStruct(shape, jnp.bfloat16),
        grid=(width // step,),
        in_specs=[
            pl.BlockSpec((height, depth), lambda j: (0, 0)),
            pl.BlockSpec((depth, step), lambda j: (0, j)),
            pl.BlockSpec((height // BLK, step), lambda j: (0, base + j)),
        ]
        + [pl.BlockSpec(memory_space=pl.ANY)] * len(extra),
        out_specs=pl.BlockSpec((height, step), lambda j: (0, base + j)),
        input_output_aliases={3: 0} if extra else {},
        compiler_params=pltpu.CompilerParams(vmem_limit_bytes=24 * 2**20),
        cost_estimate=pl.CostEstimate(
            flops=2 * height * depth * width, bytes_accessed=2 * height * width, transcendentals=0
        ),
    )(rows_t, delta, mask, *extra)


def line_gradient(hidden, rows, mask, into, shape, first):
    depth, width = hidden.shape
    breadth = rows.shape[1]
    step = min(256, width)
    base = first // step
    extra = [] if into is None else [into]
    return pl.pallas_call(
        functools.partial(gradient_kernel, True),
        out_shape=jax.ShapeDtypeStruct(shape, jnp.bfloat16),
        grid=(width // step,),
        in_specs=[
            pl.BlockSpec((depth, step), lambda j: (0, j)),
            pl.BlockSpec((depth, breadth), lambda j: (0, 0)),
            pl.BlockSpec((step // BLK, 1, breadth), lambda j: (base + j, 0, 0)),
        ]
        + [pl.BlockSpec(memory_space=pl.ANY)] * len(extra),
        out_specs=pl.BlockSpec((step, breadth), lambda j: (base + j, 0)),
        input_output_aliases={3: 0} if extra else {},
        compiler_params=pltpu.CompilerParams(vmem_limit_bytes=24 * 2**20),
        cost_estimate=pl.CostEstimate(
            flops=2 * depth * width * breadth, bytes_accessed=2 * width * breadth, transcendentals=0
        ),
    )(hidden, rows, mask[:, None, :], *extra)


def on_device(n_row, n_col, tokens, cotangent, gate_weight, up_weight, down_weight, gate_keep, down_keep):
    core = lax.rem(lax.axis_index("row"), 2)
    chips = n_row // 2
    swap = [(i, i ^ 1) for i in range(n_row)]
    height, width = gate_weight.shape
    own_rows = tokens.shape[0]
    size = min(1024, width)
    chunks = width // size

    def across(value):
        total = value.astype(jnp.float32)
        for k in range(1, chips):
            pairs = [(i, (i + 2 * k) % n_row) for i in range(n_row)]
            total = total + lax.ppermute(value, "row", pairs).astype(jnp.float32)
        return total

    def core_order(value):
        half = value.shape[1] // 2
        mine = lax.dynamic_slice_in_dim(value, core * half, half, 1)
        theirs = lax.dynamic_slice_in_dim(value, (1 - core) * half, half, 1)
        return jnp.concatenate([mine, theirs], axis=1)

    both = jnp.stack([tokens, cotangent])
    blocks = []
    for s in range(1, n_col):
        blocks.append(lax.ppermute(both, "col", [(i, (i + s) % n_col) for i in range(n_col)]))
    own = core_order(both)
    groups = [own]
    if blocks:
        groups.append(jnp.concatenate([core_order(b)[:, : own_rows // 2] for b in blocks] + [core_order(b)[:, own_rows // 2 :] for b in blocks], axis=1))
    rows = jnp.concatenate(groups, axis=1)
    tokens_t = rows[0].T

    gate_lines = widen(gate_keep, 1)
    down_lines = widen(down_keep, 1)
    gate_lines_wide = gate_lines.astype(jnp.float32)
    down_lines_wide = down_lines.astype(jnp.float32)

    weights = []
    for k in range(chunks):
        lower = k * size
        lines = gate_lines[:, lower : lower + size]
        weights.append(
            (
                masked(gate_weight[:, lower : lower + size], lines),
                masked(up_weight[:, lower : lower + size], lines),
                masked(down_weight[lower : lower + size], down_lines[lower // BLK : (lower + size) // BLK]),
            )
        )

    def unit(g, k):
        x, (gate, up, down) = groups[g], weights[k]
        half = x.shape[1] // 2
        whole = jnp.stack([ahead(x[0], gate), ahead(x[0], up), behind(x[1], down)]).astype(jnp.bfloat16)
        came = lax.ppermute(whole[:, half:], "row", swap)
        mine = (whole[:, :half].astype(jnp.float32) + came.astype(jnp.float32)).astype(jnp.bfloat16)
        result = deltas(across(mine))
        return jnp.concatenate([result, lax.ppermute(result, "row", swap)], axis=1)

    early = max(1, chunks - 1)
    order = [(0, k) for k in range(early)] + [(g, k) for g in range(1, len(groups)) for k in range(chunks)] + [(0, k) for k in range(early, chunks)]
    outs = {}
    for g, k in order:
        outs[g, k] = unit(g, k)

    gate_gradient = up_gradient = down_gradient = None
    terms = [0.0] * len(groups)
    for k in range(chunks):
        gate, up, down = weights[k]
        for g in range(len(groups)):
            terms[g] = terms[g] + behind(outs[g, k][1], gate) + behind(outs[g, k][2], up)
        h = jnp.concatenate([outs[g, k] for g in range(len(groups))], axis=1)
        gate_gradient = column_gradient(tokens_t, h[1], gate_lines_wide, gate_gradient, gate_weight.shape, k * size)
        up_gradient = column_gradient(tokens_t, h[2], gate_lines_wide, up_gradient, up_weight.shape, k * size)
        down_gradient = line_gradient(h[0], rows[1], down_lines_wide, down_gradient, down_weight.shape, k * size)

    total = terms[0]
    half = own_rows // 2
    if blocks:
        other = terms[1].astype(jnp.bfloat16)
        middle = half * len(blocks)
        for s in range(1, n_col):
            at = (s - 1) * half
            block = jnp.concatenate([other[at : at + half], other[middle + at : middle + at + half]], axis=0)
            total = total + lax.ppermute(block, "col", [(i, (i - s) % n_col) for i in range(n_col)]).astype(jnp.float32)
    restored = core_order(total[None])[0]
    return (restored.astype(jnp.bfloat16), gate_gradient, up_gradient, down_gradient)


def solution(mesh):
    placed = (
        P(("groups", "col"), "row"),
        P(("groups", "col"), "row"),
        P("row", "col"),
        P("row", "col"),
        P("col", "row"),
        P("row", "col"),
        P("col", "row"),
    )
    return jax.shard_map(
        functools.partial(on_device, mesh.shape["row"], mesh.shape["col"]),
        mesh=mesh,
        in_specs=placed,
        out_specs=(
            P(("groups", "col"), "row"),
            P(("groups", "row"), "col"),
            P(("groups", "row"), "col"),
            P(("groups", "col"), "row"),
        ),
        check_vma=False,
    )
```

```python
import functools

import jax
import jax.numpy as jnp
from jax import lax
from jax.experimental import pallas as pl
from jax.experimental.pallas import tpu as pltpu
from jax.sharding import PartitionSpec as P

BLK = 128
STEP = 256
CONTRACT_ROWS = (((0,), (0,)), ((), ()))
CONTRACT_COLUMNS = (((1,), (1,)), ((), ()))
PARAMS = pltpu.CompilerParams(vmem_limit_bytes=40 * 2**20)


def masked(weight, lines):
    rows, columns = weight.shape
    blocked = weight.reshape(rows // BLK, BLK, columns) * lines
    return blocked.reshape(rows, columns)


def ahead(left, weight):
    return jnp.dot(left, weight, preferred_element_type=jnp.float32)


def behind(left, weight):
    return lax.dot_general(left, weight, CONTRACT_COLUMNS, preferred_element_type=jnp.float32)


def outer(left, right):
    return lax.dot_general(left, right, CONTRACT_ROWS, preferred_element_type=jnp.float32)


def cost(flops, moved):
    return pl.CostEstimate(flops=flops, bytes_accessed=moved, transcendentals=0)


ANY = pl.BlockSpec(memory_space=pl.ANY)


def product_kernel(x_ref, g_ref, u_ref, d_ref, gl_ref, dl_ref, *refs):
    mine_ref, theirs_ref = refs[-2:]
    half = mine_ref.shape[1]
    tokens, cotangent = x_ref[0], x_ref[1]

    def put(i, value):
        value = value.astype(jnp.bfloat16)
        mine_ref[i] = value[:half]
        theirs_ref[i] = value[half:]

    put(0, ahead(tokens, masked(g_ref[...], gl_ref[...])))
    put(1, ahead(tokens, masked(u_ref[...], gl_ref[...])))
    put(2, behind(cotangent, masked(d_ref[...], dl_ref[...])))


def products(x, weights, lines, k, size, after):
    gate, up, down = weights
    count, height = x.shape[1:]
    step = min(STEP, size)
    base = k * size // step
    out = jax.ShapeDtypeStruct((3, count // 2, size), jnp.bfloat16)
    columns = pl.BlockSpec((height, step), lambda j: (0, base + j))
    return pl.pallas_call(
        product_kernel,
        out_shape=(out, out),
        grid=(size // step,),
        in_specs=[
            pl.BlockSpec((2, count, height), lambda j: (0, 0, 0)),
            columns,
            columns,
            pl.BlockSpec((step, height), lambda j: (base + j, 0)),
            pl.BlockSpec((height // BLK, 1, step), lambda j: (0, 0, base + j)),
            pl.BlockSpec((step // BLK, 1, height), lambda j: (base + j, 0, 0)),
        ]
        + [ANY] * len(after),
        out_specs=[pl.BlockSpec((3, count // 2, step), lambda j: (0, 0, j))] * 2,
        compiler_params=PARAMS,
        cost_estimate=cost(6 * count * height * size, 6 * height * size),
    )(x, gate, up, down, *lines, *after)


def delta_kernel(n, *refs):
    out_ref = refs[-1]
    gate, up, hidden_delta = (
        functools.reduce(lambda a, b: a + b, [r[i].astype(jnp.float32) for r in refs[:n]]) for i in range(3)
    )
    sigma = jax.nn.sigmoid(gate)
    active = gate * sigma
    out_ref[0] = (active * up).astype(jnp.bfloat16)
    out_ref[1] = (hidden_delta * up * sigma * (1.0 + gate * (1.0 - sigma))).astype(jnp.bfloat16)
    out_ref[2] = (hidden_delta * active).astype(jnp.bfloat16)


def deltas(parts, after):
    three, count, size = parts[0].shape
    step = min(STEP, size)
    spec = pl.BlockSpec((three, count, step), lambda j: (0, 0, j))
    return pl.pallas_call(
        functools.partial(delta_kernel, len(parts)),
        out_shape=jax.ShapeDtypeStruct(parts[0].shape, jnp.bfloat16),
        grid=(size // step,),
        in_specs=[spec] * len(parts) + [ANY] * len(after),
        out_specs=spec,
        compiler_params=PARAMS,
        cost_estimate=cost(60 * count * size, 18 * count * size),
    )(*parts, *after)


def term_kernel(first, *refs):
    gd_mine, gd_theirs, ud_mine, ud_theirs, g_ref, u_ref, l_ref = refs[:7]
    out_ref = refs[-1]
    gate_delta = jnp.concatenate([gd_mine[0], gd_theirs[0]], axis=0)
    up_delta = jnp.concatenate([ud_mine[0], ud_theirs[0]], axis=0)
    value = behind(gate_delta, masked(g_ref[...], l_ref[...])) + behind(up_delta, masked(u_ref[...], l_ref[...]))
    out_ref[...] = value if first else refs[7][...] + value


def add_term(pair, weights, lines, k, size, term):
    gate, up, _ = weights
    height = gate.shape[0]
    count = 2 * pair[0].shape[1]
    step = min(STEP, height)
    held = pl.BlockSpec((count, step), lambda j: (0, j))
    rows = pl.BlockSpec((step, size), lambda j: (j, k))
    pieces = [pl.BlockSpec((1, count // 2, size), lambda j, i=i: (i, 0, 0)) for i in (1, 1, 2, 2)]
    extra = [] if term is None else [term]
    return pl.pallas_call(
        functools.partial(term_kernel, term is None),
        out_shape=jax.ShapeDtypeStruct((count, height), jnp.float32),
        grid=(height // step,),
        in_specs=pieces
        + [rows, rows, pl.BlockSpec((step // BLK, 1, size), lambda j: (j, 0, k))]
        + [held] * len(extra),
        out_specs=held,
        compiler_params=PARAMS,
        cost_estimate=cost(4 * count * height * size, 4 * height * size),
    )(pair[0], pair[1], pair[0], pair[1], gate, up, lines[0], *extra)


def gradient_kernel(n, *refs):
    parts = refs[:n]
    tokens_ref, cotangent_ref, gl_ref, dl_ref = refs[n : n + 4]
    gate_ref, up_ref, down_ref = refs[-3:]

    def put(ref, product, lines):
        rows, columns = product.shape
        blocked = product.reshape(rows // BLK, BLK, columns) * lines.astype(jnp.float32)
        ref[...] = blocked.reshape(rows, columns).astype(jnp.bfloat16)

    hidden, gate_delta, up_delta = (jnp.concatenate([p[i] for p in parts], axis=0) for i in range(3))
    put(gate_ref, ahead(tokens_ref[...], gate_delta), gl_ref[...])
    put(up_ref, ahead(tokens_ref[...], up_delta), gl_ref[...])
    put(down_ref, outer(hidden, cotangent_ref[...]), dl_ref[...])


def gradients(parts, tokens_t, cotangent, lines, k, size, width, into):
    height, depth = tokens_t.shape
    step = min(STEP, size)
    base = k * size // step
    n = len(parts)
    columns = pl.BlockSpec((height, step), lambda j: (0, base + j))
    down_rows = pl.BlockSpec((step, height), lambda j: (base + j, 0))
    wide = jax.ShapeDtypeStruct((height, width), jnp.bfloat16)
    return pl.pallas_call(
        functools.partial(gradient_kernel, n),
        out_shape=(wide, wide, jax.ShapeDtypeStruct((width, height), jnp.bfloat16)),
        grid=(size // step,),
        in_specs=[pl.BlockSpec((3, p.shape[1], step), lambda j: (0, 0, j)) for p in parts]
        + [
            pl.BlockSpec((height, depth), lambda j: (0, 0)),
            pl.BlockSpec((depth, height), lambda j: (0, 0)),
            pl.BlockSpec((height // BLK, 1, step), lambda j: (0, 0, base + j)),
            pl.BlockSpec((step // BLK, 1, height), lambda j: (base + j, 0, 0)),
        ]
        + [ANY] * len(into),
        out_specs=(columns, columns, down_rows),
        input_output_aliases={n + 4 + i: i for i in range(len(into))},
        compiler_params=PARAMS,
        cost_estimate=cost(6 * height * depth * size, 6 * height * size),
    )(*parts, tokens_t, cotangent, *lines, *into)


def on_device(n_row, n_col, tokens, cotangent, gate_weight, up_weight, down_weight, gate_keep, down_keep):
    core = lax.rem(lax.axis_index("row"), 2)
    chips = n_row // 2
    swap = [(i, i ^ 1) for i in range(n_row)]
    height, width = gate_weight.shape
    own_rows = tokens.shape[0]
    half = own_rows // 2
    size = min(1024, width)
    chunks = width // size
    weights = (gate_weight, up_weight, down_weight)
    lines = tuple(jnp.repeat(keep, BLK, axis=1).astype(jnp.bfloat16)[:, None, :] for keep in (gate_keep, down_keep))

    def core_order(value):
        return jnp.where(core == 0, value, jnp.concatenate([value[:, half:], value[:, :half]], axis=1))

    def shifted(value, s):
        return lax.ppermute(value, "col", [(i, (i + s) % n_col) for i in range(n_col)])

    both = core_order(jnp.stack([tokens, cotangent]))
    block = {0: both}
    for s in range(1, n_col // 2 + 1):
        block[s] = shifted(block[s - 1], 1)
        if n_col - s > n_col // 2:
            block[n_col - s] = shifted(block[(n_col - s + 1) % n_col], -1)
    near = [s for s in dict.fromkeys((1, n_col - 1)) if 0 < s < n_col]
    far = [s for s in range(2, n_col - 1)]
    shifts = [g for g in ([0], near, far) if g]
    groups = [
        jnp.concatenate([block[s][:, :half] for s in g] + [block[s][:, half:] for s in g], axis=1) for g in shifts
    ]
    rows = jnp.concatenate(groups, axis=1)
    tokens_t = rows[0].T

    order = [(0, k) for k in range(chunks)]
    if len(groups) > 1:
        order += [(1, 0)] + [(1, 1)] * (chunks > 1)
    if len(groups) > 2:
        for k in range(chunks):
            order += [(2, k)] + [(1, k + 2)] * (k + 2 < chunks)
    elif len(groups) > 1:
        order += [(1, k) for k in range(2, chunks)]

    mine_of, pairs, terms = [], {}, [None] * len(groups)
    seen, into, ready = [0] * chunks, (), {}
    for at, (g, k) in enumerate(order):
        after = [mine_of[at - 2]] if at >= 2 else []
        mine, theirs = products(groups[g], weights, lines, k, size, after)
        came = lax.ppermute(theirs, "row", swap)
        mine = (mine.astype(jnp.float32) + came.astype(jnp.float32)).astype(jnp.bfloat16)
        mine_of.append(mine)
        parts = [mine]
        for c in range(1, chips):
            parts.append(lax.ppermute(mine, "row", [(i, (i + 2 * c) % n_row) for i in range(n_row)]))
        result = deltas(parts, ready.get(at, []))
        pairs[g, k] = (result, lax.ppermute(result, "row", swap))
        terms[g] = add_term(pairs[g, k], weights, lines, k, size, terms[g])
        done = [terms[g]]
        seen[k] += 1
        if seen[k] == len(groups):
            pieces = [p for gg in range(len(groups)) for p in pairs[gg, k]]
            into = gradients(pieces, tokens_t, rows[1], lines, k, size, width, into)
            done += list(into)
        ready[at + 2] = done

    total = terms[0]
    for g in range(1, len(groups)):
        sent = terms[g].astype(jnp.bfloat16)
        middle = half * len(shifts[g])
        for at, s in enumerate(shifts[g]):
            low = at * half
            piece = jnp.concatenate([sent[low : low + half], sent[middle + low : middle + low + half]], axis=0)
            total = total + shifted(piece, -s).astype(jnp.float32)
    return (core_order(total[None])[0].astype(jnp.bfloat16), *into)


def solution(mesh):
    placed = (
        P(("groups", "col"), "row"),
        P(("groups", "col"), "row"),
        P("row", "col"),
        P("row", "col"),
        P("col", "row"),
        P("row", "col"),
        P("col", "row"),
    )
    return jax.shard_map(
        functools.partial(on_device, mesh.shape["row"], mesh.shape["col"]),
        mesh=mesh,
        in_specs=placed,
        out_specs=(
            P(("groups", "col"), "row"),
            P(("groups", "row"), "col"),
            P(("groups", "row"), "col"),
            P(("groups", "col"), "row"),
        ),
        check_vma=False,
    )
```

```python
import functools

import jax
import jax.numpy as jnp
from jax import lax
from jax.experimental import pallas as pl
from jax.experimental.pallas import tpu as pltpu
from jax.sharding import PartitionSpec as P

BLK = 128
STEP = 256
CONTRACT_ROWS = (((0,), (0,)), ((), ()))
CONTRACT_COLUMNS = (((1,), (1,)), ((), ()))
PARAMS = pltpu.CompilerParams(vmem_limit_bytes=56 * 2**20)


def masked(weight, lines):
    rows, columns = weight.shape
    blocked = weight.reshape(rows // BLK, BLK, columns) * lines
    return blocked.reshape(rows, columns)


def ahead(left, weight):
    return jnp.dot(left, weight, preferred_element_type=jnp.float32)


def behind(left, weight):
    return lax.dot_general(left, weight, CONTRACT_COLUMNS, preferred_element_type=jnp.float32)


def outer(left, right):
    return lax.dot_general(left, right, CONTRACT_ROWS, preferred_element_type=jnp.float32)


def cost(flops, moved):
    return pl.CostEstimate(flops=flops, bytes_accessed=moved, transcendentals=0)


ANY = pl.BlockSpec(memory_space=pl.ANY)


def product_kernel(x_ref, g_ref, u_ref, d_ref, gl_ref, dl_ref, *refs):
    mine_ref, theirs_ref = refs[-2:]
    half = mine_ref.shape[1]
    tokens, cotangent = x_ref[0], x_ref[1]

    def put(i, value):
        value = value.astype(jnp.bfloat16)
        mine_ref[i] = value[:half]
        theirs_ref[i] = value[half:]

    put(0, ahead(tokens, masked(g_ref[...], gl_ref[...])))
    put(1, ahead(tokens, masked(u_ref[...], gl_ref[...])))
    put(2, behind(cotangent, masked(d_ref[...], dl_ref[...])))


def products(x, weights, lines, k, size, after):
    gate, up, down = weights
    count, height = x.shape[1:]
    step = min(STEP, size)
    base = k * size // step
    out = jax.ShapeDtypeStruct((3, count // 2, size), jnp.bfloat16)
    columns = pl.BlockSpec((height, step), lambda j: (0, base + j))
    return pl.pallas_call(
        product_kernel,
        out_shape=(out, out),
        grid=(size // step,),
        in_specs=[
            pl.BlockSpec((2, count, height), lambda j: (0, 0, 0)),
            columns,
            columns,
            pl.BlockSpec((step, height), lambda j: (base + j, 0)),
            pl.BlockSpec((height // BLK, 1, step), lambda j: (0, 0, base + j)),
            pl.BlockSpec((step // BLK, 1, height), lambda j: (base + j, 0, 0)),
        ]
        + [ANY] * len(after),
        out_specs=[pl.BlockSpec((3, count // 2, step), lambda j: (0, 0, j))] * 2,
        compiler_params=PARAMS,
        cost_estimate=cost(6 * count * height * size, 6 * height * size),
    )(x, gate, up, down, *lines, *after)


def join_kernel(n, *refs):
    out_ref = refs[-1]
    half = refs[0].shape[1] // 2
    for i in range(n):
        out_ref[:, i * half : (i + 1) * half] = refs[i][:, :half]
        out_ref[:, (n + i) * half : (n + i + 1) * half] = refs[i][:, half:]


def joined(blocks, after):
    n = len(blocks)
    two, count, height = blocks[0].shape
    step = min(2 * STEP, height)
    return pl.pallas_call(
        functools.partial(join_kernel, n),
        out_shape=jax.ShapeDtypeStruct((two, n * count, height), jnp.bfloat16),
        grid=(height // step,),
        in_specs=[pl.BlockSpec((two, count, step), lambda j: (0, 0, j))] * n + [ANY] * len(after),
        out_specs=pl.BlockSpec((two, n * count, step), lambda j: (0, 0, j)),
        compiler_params=PARAMS,
        cost_estimate=cost(0, 4 * n * two * count * height),
    )(*blocks, *after)


def add_kernel(left_ref, right_ref, *refs):
    out_ref = refs[-1]
    out_ref[...] = (left_ref[...].astype(jnp.float32) + right_ref[...].astype(jnp.float32)).astype(jnp.bfloat16)


def added(left, right, after):
    three, count, size = left.shape
    step = min(2 * STEP, size)
    spec = pl.BlockSpec((three, count, step), lambda j: (0, 0, j))
    return pl.pallas_call(
        add_kernel,
        out_shape=jax.ShapeDtypeStruct(left.shape, jnp.bfloat16),
        grid=(size // step,),
        in_specs=[spec] * 2 + [ANY] * len(after),
        out_specs=spec,
        compiler_params=PARAMS,
        cost_estimate=cost(3 * count * size, 18 * count * size),
    )(left, right, *after)


def delta_kernel(n, *refs):
    out_ref = refs[-1]
    gate, up, hidden_delta = (
        functools.reduce(lambda a, b: a + b, [r[i].astype(jnp.float32) for r in refs[:n]]) for i in range(3)
    )
    sigma = jax.nn.sigmoid(gate)
    active = gate * sigma
    out_ref[0] = (active * up).astype(jnp.bfloat16)
    out_ref[1] = (hidden_delta * up * sigma * (1.0 + gate * (1.0 - sigma))).astype(jnp.bfloat16)
    out_ref[2] = (hidden_delta * active).astype(jnp.bfloat16)


def deltas(parts, after):
    three, count, size = parts[0].shape
    step = min(STEP, size)
    spec = pl.BlockSpec((three, count, step), lambda j: (0, 0, j))
    return pl.pallas_call(
        functools.partial(delta_kernel, len(parts)),
        out_shape=jax.ShapeDtypeStruct(parts[0].shape, jnp.bfloat16),
        grid=(size // step,),
        in_specs=[spec] * len(parts) + [ANY] * len(after),
        out_specs=spec,
        compiler_params=PARAMS,
        cost_estimate=cost(60 * count * size, 18 * count * size),
    )(*parts, *after)


def term_kernel(first, n, *refs):
    g_ref, u_ref, l_ref = refs[2 * n : 2 * n + 3]
    out_ref = refs[-1]
    gate_delta = jnp.concatenate([r[0] for r in refs[:n]], axis=0)
    up_delta = jnp.concatenate([r[0] for r in refs[n : 2 * n]], axis=0)
    value = behind(gate_delta, masked(g_ref[...], l_ref[...])) + behind(up_delta, masked(u_ref[...], l_ref[...]))
    out_ref[...] = value if first else refs[2 * n + 3][...] + value


def add_term(parts, weights, lines, k, size, term, after):
    gate, up, _ = weights
    height = gate.shape[0]
    count = sum(p.shape[1] for p in parts)
    step = min(STEP, height)
    held = pl.BlockSpec((count, step), lambda j: (0, j))
    rows = pl.BlockSpec((step, size), lambda j: (j, k))
    pieces = [pl.BlockSpec((1, p.shape[1], size), lambda j, i=i: (i, 0, 0)) for i in (1, 2) for p in parts]
    extra = [] if term is None else [term]
    return pl.pallas_call(
        functools.partial(term_kernel, term is None, len(parts)),
        out_shape=jax.ShapeDtypeStruct((count, height), jnp.float32),
        grid=(height // step,),
        in_specs=pieces
        + [rows, rows, pl.BlockSpec((step // BLK, 1, size), lambda j: (j, 0, k))]
        + [held] * len(extra)
        + [ANY] * len(after),
        out_specs=held,
        compiler_params=PARAMS,
        cost_estimate=cost(4 * count * height * size, 4 * height * size),
    )(*parts, *parts, gate, up, lines[0], *extra, *after)


def gradient_kernel(n, *refs):
    parts = refs[:n]
    tokens_ref, cotangent_ref, gl_ref, dl_ref = refs[n : n + 4]
    gate_ref, up_ref, down_ref, token_ref = refs[-4:]
    token_ref[...] = jnp.zeros_like(token_ref)

    def put(ref, product, lines):
        rows, columns = product.shape
        blocked = product.reshape(rows // BLK, BLK, columns) * lines.astype(jnp.float32)
        ref[...] = blocked.reshape(rows, columns).astype(jnp.bfloat16)

    hidden, gate_delta, up_delta = (jnp.concatenate([p[i] for p in parts], axis=0) for i in range(3))
    put(gate_ref, ahead(tokens_ref[...], gate_delta), gl_ref[...])
    put(up_ref, ahead(tokens_ref[...], up_delta), gl_ref[...])
    put(down_ref, outer(hidden, cotangent_ref[...]), dl_ref[...])


def gradients(parts, tokens_t, cotangent, lines, k, size, width, into, after):
    height, depth = tokens_t.shape
    step = min(STEP, size)
    base = k * size // step
    n = len(parts)
    columns = pl.BlockSpec((height, step), lambda j: (0, base + j))
    down_rows = pl.BlockSpec((step, height), lambda j: (base + j, 0))
    wide = jax.ShapeDtypeStruct((height, width), jnp.bfloat16)
    return pl.pallas_call(
        functools.partial(gradient_kernel, n),
        out_shape=(wide, wide, jax.ShapeDtypeStruct((width, height), jnp.bfloat16), jax.ShapeDtypeStruct((8, BLK), jnp.float32)),
        grid=(size // step,),
        in_specs=[pl.BlockSpec((3, p.shape[1], step), lambda j: (0, 0, j)) for p in parts]
        + [
            pl.BlockSpec((height, depth), lambda j: (0, 0)),
            pl.BlockSpec((depth, height), lambda j: (0, 0)),
            pl.BlockSpec((height // BLK, 1, step), lambda j: (0, 0, base + j)),
            pl.BlockSpec((step // BLK, 1, height), lambda j: (base + j, 0, 0)),
        ]
        + [ANY] * (len(into) + len(after)),
        out_specs=(columns, columns, down_rows, pl.BlockSpec((8, BLK), lambda j: (0, 0))),
        input_output_aliases={n + 4 + i: i for i in range(len(into))},
        compiler_params=PARAMS,
        cost_estimate=cost(6 * height * depth * size, 6 * height * size),
    )(*parts, tokens_t, cotangent, *lines, *into, *after)


def on_device(n_row, n_col, tokens, cotangent, gate_weight, up_weight, down_weight, gate_keep, down_keep):
    core = lax.rem(lax.axis_index("row"), 2)
    chips = n_row // 2
    swap = [(i, i ^ 1) for i in range(n_row)]
    height, width = gate_weight.shape
    own_rows = tokens.shape[0]
    half = own_rows // 2
    size = min(1024, width)
    chunks = width // size
    weights = (gate_weight, up_weight, down_weight)
    lines = tuple(jnp.repeat(keep, BLK, axis=1).astype(jnp.bfloat16)[:, None, :] for keep in (gate_keep, down_keep))

    def core_order(value):
        return jnp.where(core == 0, value, jnp.concatenate([value[:, half:], value[:, :half]], axis=1))

    def shifted(value, s):
        return lax.ppermute(value, "col", [(i, (i + s) % n_col) for i in range(n_col)])

    both = core_order(jnp.stack([tokens, cotangent]))
    others = [shifted(both, s) for s in range(1, n_col)]
    groups = [both]

    last = []

    def chained(kernel, *operands):
        result = kernel(*operands, list(last))
        last[:] = [result[-1] if isinstance(result, (tuple, list)) else result]
        return result

    pending, summed, pairs = {}, {}, {}

    def multiply(u):
        g, k = u
        mine, theirs = chained(products, groups[g], weights, lines, k, size)
        pending[u] = (mine, lax.ppermute(theirs, "row", swap))

    def combine(u):
        mine = chained(added, *pending[u])
        summed[u] = [mine]
        for c in range(1, chips):
            summed[u].append(lax.ppermute(mine, "row", [(i, (i + 2 * c) % n_row) for i in range(n_row)]))

    def activate(u):
        result = chained(deltas, summed[u])
        pairs[u] = (result, lax.ppermute(result, "row", swap))

    own = [(0, k) for k in range(chunks)]
    rest = [(1, k) for k in range(chunks)] if others else []
    for i in range(chunks + 1):
        if i < chunks:
            multiply(own[i])
        if i > 0:
            combine(own[i - 1])
    for u in own[:-1]:
        activate(u)
    if rest:
        groups.append(chained(joined, others))
        multiply(rest[0])
        for i in range(1, chunks + 1):
            if i < chunks:
                multiply(rest[i])
            combine(rest[i - 1])
    for u in own[-1:]:
        if u not in pairs:
            activate(u)
    rows = jnp.concatenate(groups, axis=1)
    tokens_t = rows[0].T
    term, into = None, ()
    for k in range(chunks):
        if rest:
            activate(rest[k])
        pieces = [p for g in range(len(groups)) for p in pairs[g, k]]
        term = chained(add_term, pieces, weights, lines, k, size, term)
        *into, _ = chained(gradients, pieces, tokens_t, rows[1], lines, k, size, width, into)

    total = term[:own_rows]
    sent = term[own_rows:].astype(jnp.bfloat16)
    middle = half * len(others)
    for s in range(1, n_col):
        low = (s - 1) * half
        piece = jnp.concatenate([sent[low : low + half], sent[middle + low : middle + low + half]], axis=0)
        total = total + shifted(piece, -s).astype(jnp.float32)
    return (core_order(total[None])[0].astype(jnp.bfloat16), *into)


def solution(mesh):
    placed = (
        P(("groups", "col"), "row"),
        P(("groups", "col"), "row"),
        P("row", "col"),
        P("row", "col"),
        P("col", "row"),
        P("row", "col"),
        P("col", "row"),
    )
    return jax.shard_map(
        functools.partial(on_device, mesh.shape["row"], mesh.shape["col"]),
        mesh=mesh,
        in_specs=placed,
        out_specs=(
            P(("groups", "col"), "row"),
            P(("groups", "row"), "col"),
            P(("groups", "row"), "col"),
            P(("groups", "col"), "row"),
        ),
        check_vma=False,
    )
```

```python
import functools

import jax
import jax.numpy as jnp
from jax import lax
from jax.experimental import pallas as pl
from jax.experimental.pallas import tpu as pltpu
from jax.sharding import PartitionSpec as P

BLK = 128
STEP = 256
CONTRACT_ROWS = (((0,), (0,)), ((), ()))
CONTRACT_COLUMNS = (((1,), (1,)), ((), ()))
PARAMS = pltpu.CompilerParams(vmem_limit_bytes=40 * 2**20)


def widen(keep, axis):
    return jnp.repeat(keep, BLK, axis=axis).astype(jnp.bfloat16)


def masked(weight, lines):
    rows, columns = weight.shape
    blocked = weight.reshape(rows // BLK, BLK, columns) * lines[:, None, :]
    return blocked.reshape(rows, columns)


def ahead(left, weight):
    return jnp.dot(left, weight, preferred_element_type=jnp.float32)


def behind(left, weight):
    return lax.dot_general(left, weight, CONTRACT_COLUMNS, preferred_element_type=jnp.float32)


def outer(left, right):
    return lax.dot_general(left, right, CONTRACT_ROWS, preferred_element_type=jnp.float32)


def cost(flops, moved):
    return pl.CostEstimate(flops=flops, bytes_accessed=moved, transcendentals=0)


ANY = pl.BlockSpec(memory_space=pl.ANY)


def delta_kernel(n, *refs):
    out_ref = refs[-1]
    gate, up, hidden_delta = (
        functools.reduce(lambda a, b: a + b, [r[i].astype(jnp.float32) for r in refs[:n]]) for i in range(3)
    )
    sigma = jax.nn.sigmoid(gate)
    active = gate * sigma
    out_ref[0] = (active * up).astype(jnp.bfloat16)
    out_ref[1] = (hidden_delta * up * sigma * (1.0 + gate * (1.0 - sigma))).astype(jnp.bfloat16)
    out_ref[2] = (hidden_delta * active).astype(jnp.bfloat16)


def deltas(parts, after):
    three, count, size = parts[0].shape
    step = min(STEP, size)
    spec = pl.BlockSpec((three, count, step), lambda j: (0, 0, j))
    return pl.pallas_call(
        functools.partial(delta_kernel, len(parts)),
        out_shape=jax.ShapeDtypeStruct(parts[0].shape, jnp.bfloat16),
        grid=(size // step,),
        in_specs=[spec] * len(parts) + [ANY] * len(after),
        out_specs=spec,
        compiler_params=PARAMS,
        cost_estimate=cost(60 * count * size, 18 * count * size),
    )(*parts, *after)


def gradient_kernel(n, *refs):
    parts = refs[:n]
    tokens_ref, cotangent_ref, gl_ref, dl_ref = refs[n : n + 4]
    gate_ref, up_ref, down_ref, token_ref = refs[-4:]
    token_ref[...] = jnp.zeros_like(token_ref)

    def put(ref, product, lines):
        rows, columns = product.shape
        blocked = product.reshape(rows // BLK, BLK, columns) * lines.astype(jnp.float32)
        ref[...] = blocked.reshape(rows, columns).astype(jnp.bfloat16)

    hidden, gate_delta, up_delta = (jnp.concatenate([p[i] for p in parts], axis=0) for i in range(3))
    put(gate_ref, ahead(tokens_ref[...], gate_delta), gl_ref[...])
    put(up_ref, ahead(tokens_ref[...], up_delta), gl_ref[...])
    put(down_ref, outer(hidden, cotangent_ref[...]), dl_ref[...])


def gradients(parts, tokens_t, cotangent, lines, k, size, width, into, after):
    height, depth = tokens_t.shape
    step = min(STEP, size)
    base = k * size // step
    n = len(parts)
    columns = pl.BlockSpec((height, step), lambda j: (0, base + j))
    down_rows = pl.BlockSpec((step, height), lambda j: (base + j, 0))
    wide = jax.ShapeDtypeStruct((height, width), jnp.bfloat16)
    return pl.pallas_call(
        functools.partial(gradient_kernel, n),
        out_shape=(wide, wide, jax.ShapeDtypeStruct((width, height), jnp.bfloat16), jax.ShapeDtypeStruct((8, BLK), jnp.float32)),
        grid=(size // step,),
        in_specs=[pl.BlockSpec((3, p.shape[1], step), lambda j: (0, 0, j)) for p in parts]
        + [
            pl.BlockSpec((height, depth), lambda j: (0, 0)),
            pl.BlockSpec((depth, height), lambda j: (0, 0)),
            pl.BlockSpec((height // BLK, 1, step), lambda j: (0, 0, base + j)),
            pl.BlockSpec((step // BLK, 1, height), lambda j: (base + j, 0, 0)),
        ]
        + [ANY] * (len(into) + len(after)),
        out_specs=(columns, columns, down_rows, pl.BlockSpec((8, BLK), lambda j: (0, 0))),
        input_output_aliases={n + 4 + i: i for i in range(len(into))},
        compiler_params=PARAMS,
        cost_estimate=cost(6 * height * depth * size, 6 * height * size),
    )(*parts, tokens_t, cotangent, *lines, *into, *after)


def on_device(n_row, n_col, tokens, cotangent, gate_weight, up_weight, down_weight, gate_keep, down_keep):
    core = lax.rem(lax.axis_index("row"), 2)
    chips = n_row // 2
    swap = [(i, i ^ 1) for i in range(n_row)]
    height, width = gate_weight.shape
    own_rows = tokens.shape[0]
    size = min(1024, width)
    chunks = width // size

    def across(value):
        parts = [value]
        for k in range(1, chips):
            parts.append(lax.ppermute(value, "row", [(i, (i + 2 * k) % n_row) for i in range(n_row)]))
        return parts

    def core_order(value):
        half = value.shape[1] // 2
        mine = lax.dynamic_slice_in_dim(value, core * half, half, 1)
        theirs = lax.dynamic_slice_in_dim(value, (1 - core) * half, half, 1)
        return jnp.concatenate([mine, theirs], axis=1)

    both = jnp.stack([tokens, cotangent])
    blocks = []
    for s in range(1, n_col):
        blocks.append(lax.ppermute(both, "col", [(i, (i + s) % n_col) for i in range(n_col)]))
    own = core_order(both)
    groups = [own]
    if blocks:
        groups.append(jnp.concatenate([core_order(b)[:, : own_rows // 2] for b in blocks] + [core_order(b)[:, own_rows // 2 :] for b in blocks], axis=1))
    rows = jnp.concatenate(groups, axis=1)
    tokens_t = rows[0].T

    gate_lines = widen(gate_keep, 1)
    down_lines = widen(down_keep, 1)

    weights = []
    for k in range(chunks):
        lower = k * size
        lines = gate_lines[:, lower : lower + size]
        weights.append(
            (
                masked(gate_weight[:, lower : lower + size], lines),
                masked(up_weight[:, lower : lower + size], lines),
                masked(down_weight[lower : lower + size], down_lines[lower // BLK : (lower + size) // BLK]),
            )
        )

    def unit(g, k):
        x, (gate, up, down) = groups[g], weights[k]
        half = x.shape[1] // 2
        whole = jnp.stack([ahead(x[0], gate), ahead(x[0], up), behind(x[1], down)]).astype(jnp.bfloat16)
        came = lax.ppermute(whole[:, half:], "row", swap)
        mine = (whole[:, :half].astype(jnp.float32) + came.astype(jnp.float32)).astype(jnp.bfloat16)
        return across(mine)

    def finish(parts, after):
        result = deltas(parts, after)
        return result, lax.ppermute(result, "row", swap)

    order = [(g, k) for g in range(len(groups)) for k in range(chunks)]
    sums = {u: unit(*u) for u in order}
    outs = {(0, k): finish(sums[0, k], []) for k in range(chunks)}
    terms = [0.0] * len(groups)
    line_blocks = (gate_lines[:, None, :], down_lines[:, None, :])
    into, after = (), []
    for k in range(chunks):
        gate, up, down = weights[k]
        for g in range(1, len(groups)):
            outs[g, k] = finish(sums[g, k], after)
        pieces = [p for g in range(len(groups)) for p in outs[g, k]]
        for g in range(len(groups)):
            whole = jnp.concatenate(outs[g, k], axis=1)
            terms[g] = terms[g] + behind(whole[1], gate) + behind(whole[2], up)
        *into, token = gradients(pieces, tokens_t, rows[1], line_blocks, k, size, width, into, [])
        after = [token]

    total = terms[0]
    half = own_rows // 2
    if blocks:
        other = terms[1].astype(jnp.bfloat16)
        middle = half * len(blocks)
        for s in range(1, n_col):
            at = (s - 1) * half
            block = jnp.concatenate([other[at : at + half], other[middle + at : middle + at + half]], axis=0)
            total = total + lax.ppermute(block, "col", [(i, (i - s) % n_col) for i in range(n_col)]).astype(jnp.float32)
    restored = core_order(total[None])[0]
    return (restored.astype(jnp.bfloat16), *into)


def solution(mesh):
    placed = (
        P(("groups", "col"), "row"),
        P(("groups", "col"), "row"),
        P("row", "col"),
        P("row", "col"),
        P("col", "row"),
        P("row", "col"),
        P("col", "row"),
    )
    return jax.shard_map(
        functools.partial(on_device, mesh.shape["row"], mesh.shape["col"]),
        mesh=mesh,
        in_specs=placed,
        out_specs=(
            P(("groups", "col"), "row"),
            P(("groups", "row"), "col"),
            P(("groups", "row"), "col"),
            P(("groups", "col"), "row"),
        ),
        check_vma=False,
    )
```
